128 devices in a mesh: row: 8 (over y_hi, z), col: 16 (over y_lo, x, core).
Axes of the slice: x: 4, y: 4 (y_hi: 2, y_lo: 2; y = y_hi * 2 + y_lo), z: 4, core: 2. Of those that a mesh axis runs over, the one named last changes fastest.
Arguments:
- matrix: float32 [64, 64, 4096], P('row', None, 'col'), may hold values from -0.72 to 0.72
- pattern_cols: int32 [64, 16, 4], replicated, may hold values from 0 to 3, as said below
- pattern_counts: int32 [64, 16], replicated, may hold values from 0 to 4, as said below
Outputs:
- next_sign: float32 [64, 64, 4096], P('row', None, 'col')
The draws below stay inside these ranges and needn't reach their ends.
Inputs may be any that keep to these rules, and one draw needn't show every extreme that they name: `pattern_cols`: for each block row and panel the used slots name distinct block columns; unused slots hold the panel's other columns. Every block row's diagonal block is in its pattern. `pattern_counts`: some block row of every panel uses all 4 slots; a panel may hold no block of a block row. In a panel more than 2 panels away (cyclically) from a block row's own panel (block row // 4), the count is at most 1, except for at most one block row per panel.
All inputs are finite; a program needn't handle non-finite values.
Results may differ from the reference program's by a relative error of at most 0.000082.
Values sent between devices are 32-bit elements; how exact they have to be, the bound alone decides.
No kernel may reach another device: no remote copies, remote signals or barrier semaphores. Data moves between devices by JAX's collectives and lax.ppermute only.
A program may use at most 64 MiB of HBM per device.

```python
import jax
import jax.numpy as jnp
from jax import lax

BS = 64
P_SIZE = 4
S = 4
PANELS = 16
NB = 64


def draw_pattern_cols(key, part):
    key = jax.random.fold_in(key, 11)
    ranking = jax.random.randint(key, (NB, PANELS, P_SIZE), 0, 1 << 20) * P_SIZE + jnp.arange(P_SIZE, dtype=jnp.int32)
    block_rows = jnp.arange(NB, dtype=jnp.int32)[:, None, None]
    on_diagonal = (jnp.arange(PANELS, dtype=jnp.int32)[None, :, None] == block_rows // P_SIZE) & (jnp.arange(P_SIZE, dtype=jnp.int32)[None, None, :] == block_rows % P_SIZE)
    ranking = jnp.where(on_diagonal, -1, ranking)
    ordering = jnp.argsort(ranking, axis=-1, stable=True)
    return ordering[:, :, :S].astype(jnp.int32)


def draw_pattern_counts(key, part):
    key = jax.random.fold_in(key, 12)
    block_rows = jnp.arange(NB, dtype=jnp.int32)[:, None]
    panel_ids = jnp.arange(PANELS, dtype=jnp.int32)[None, :]
    ahead = (panel_ids - block_rows // P_SIZE) % PANELS
    distance = jnp.minimum(ahead, PANELS - ahead)
    home = jax.random.randint(key, (NB, PANELS), 1, S + 1)
    nearby = jax.random.randint(jax.random.fold_in(key, 2), (NB, PANELS), 0, S + 1)
    remote = (jax.random.randint(jax.random.fold_in(key, 3), (NB, PANELS), 0, 3) == 0).astype(jnp.int32)
    counts = jnp.where(distance == 0, home, jnp.where(distance <= 2, nearby, remote))
    chosen = jax.random.randint(jax.random.fold_in(key, 1), (PANELS,), 0, NB)
    return jnp.where(block_rows == chosen[None, :], S, counts).astype(jnp.int32)


def level_of(own_key, shape, shards, low, top_value):
    def one(axis_at, shards_of):
        draws = jax.random.uniform(jax.random.fold_in(jax.random.fold_in(own_key, 6), axis_at), (shards_of,), jnp.float32, low / len(shards), top_value / len(shards))
        return jnp.repeat(jnp.exp(draws), shape[axis_at] // shards_of).reshape((-1,) + (1,) * (len(shape) - axis_at - 1))

    factor_of = one(*shards[0])
    for cut in shards[1:]:
        factor_of = factor_of * one(*cut)
    return factor_of


def bell_draw(stream_key, extent, width, limit, pieces=(), kind=jnp.bfloat16):
    drawn = jax.random.normal(stream_key, extent, jnp.float32) * width
    if len(pieces) > 0:
        drawn = level_of(stream_key, extent, pieces, -0.22, 0.18) * drawn
    return jnp.clip(drawn, min=-limit, max=limit).astype(kind)


def setup_inputs(seed: int = 0) -> dict:
    keys = jax.random.split(jax.random.key(seed), 4)
    matrix = bell_draw(keys[0], (NB, BS, PANELS * S * BS), 0.12, 0.72, ((0, 8), (2, 16)), jnp.float32)
    pattern_cols = draw_pattern_cols(jax.random.fold_in(keys[3], 71), 0)
    pattern_counts = draw_pattern_counts(jax.random.fold_in(keys[3], 71), 0)
    return dict(matrix=matrix, pattern_cols=pattern_cols, pattern_counts=pattern_counts)


def placement(pattern_cols, pattern_counts):
    slot_ids = jnp.arange(S, dtype=jnp.int32)
    used = slot_ids[None, None, :] < pattern_counts[:, :, None]
    target = jnp.arange(PANELS, dtype=jnp.int32)[None, :, None] * P_SIZE + pattern_cols
    columns = jnp.arange(NB, dtype=jnp.int32)
    return ((target[..., None] == columns) & used[..., None]).astype(jnp.float32)


def reference(matrix, pattern_cols, pattern_counts):
    places = placement(pattern_cols, pattern_counts)
    blocks = matrix.reshape(NB, BS, PANELS, S, BS)
    dense_matrix = jnp.einsum("imcan,icaj->imjn", blocks, places, precision=lax.Precision.HIGHEST)
    dense_matrix = dense_matrix.reshape(NB * BS, NB * BS)
    block_mask = jnp.sum(places, axis=(1, 2))
    full_mask = jnp.repeat(jnp.repeat(block_mask, BS, axis=0), BS, axis=1)
    square = jnp.dot(dense_matrix, dense_matrix, precision=lax.Precision.HIGHEST, preferred_element_type=jnp.float32) * full_mask
    shifted = 3.0 * jnp.eye(NB * BS, dtype=jnp.float32) - square
    result = 0.5 * jnp.dot(dense_matrix, shifted, precision=lax.Precision.HIGHEST, preferred_element_type=jnp.float32) * full_mask
    slotted = jnp.einsum("imjn,icaj->imcan", result.reshape(NB, BS, NB, BS), places, precision=lax.Precision.HIGHEST)
    return slotted.reshape(NB, BS, PANELS * S * BS)
```

```python
import jax
import jax.numpy as jnp
from jax import lax
from jax.experimental import pallas as pl
from jax.experimental.pallas import tpu as pltpu
from jax.sharding import PartitionSpec as P

ROWS = 8
BS = 64
SHORT = 3
REST = ROWS - SHORT
RING = 4
SIDES = 8
VMEM = pl.BlockSpec(memory_space=pltpu.VMEM)
SMEM = pl.BlockSpec(memory_space=pltpu.SMEM)
BF16 = jnp.bfloat16
F32 = jnp.float32


def is_near(row, chip):
    ahead = (chip - row + SIDES) % SIDES
    return (ahead <= 1) | (ahead == SIDES - 1)


def chip_moves(along_row, flip, shift, near_only):
    pairs = []
    for row in range(SIDES):
        for chip in range(SIDES):
            if near_only and not is_near(row, chip):
                continue
            place = chip if along_row else row
            half, at = divmod(place, RING)
            place = (half ^ flip) * RING + (at + shift) % RING
            target = (row, place) if along_row else (place, chip)
            for core in range(2):
                pairs.append(((row * SIDES + chip) * 2 + core, (target[0] * SIDES + target[1]) * 2 + core))
    return pairs


def move(value, along_row, flip, shift, near_only=False):
    return lax.ppermute(value, ("row", "col"), chip_moves(along_row, flip, shift, near_only))


def other_core(value):
    return lax.ppermute(value, "col", [(c, c ^ 1) for c in range(2 * SIDES)])


def read_code(code):
    return [(code >> (2 * a)) & 3 for a in range(4)], code >> 8


def low_lanes():
    return lax.broadcasted_iota(jnp.int32, (1, 128), 1) < BS


def lane_mask(low, when_low, when_high):
    return jnp.where(low, when_low.astype(jnp.int32), when_high.astype(jnp.int32)) != 0


def turned(half):
    return pltpu.roll(half, BS, 1)


def spread_row(tile, code):
    cols, count = read_code(code)
    low = low_lanes()
    first, second = tile[:, :128], tile[:, 128:]
    views = [(first, 0, 1), (turned(first), 1, 0), (second, 2, 3), (turned(second), 3, 2)]
    halves = []
    for t in range(2):
        dense = jnp.zeros((BS, 128), F32)
        for view, a, b in views:
            mask = lane_mask(low, (cols[a] == 2 * t) & (count > a), (cols[b] == 2 * t + 1) & (count > b))
            dense = jnp.where(mask, view, dense)
        halves.append(dense)
    return halves


def collect_row(tile, code):
    cols, count = read_code(code)
    low = low_lanes()
    first, second = tile[:, :128], tile[:, 128:]
    views = [(first, 0, 1), (turned(first), 1, 0), (second, 2, 3), (turned(second), 3, 2)]
    halves = []
    for u in range(2):
        slots = jnp.zeros((BS, 128), F32)
        for view, j, k in views:
            mask = lane_mask(
                low, (cols[2 * u] == j) & (count > 2 * u), (cols[2 * u + 1] == k) & (count > 2 * u + 1)
            )
            slots = jnp.where(mask, view, slots)
        halves.append(slots)
    return halves


def full_row(code_ref, row, panel):
    at = jnp.int32(0)
    for i in range(ROWS):
        at = jnp.where((code_ref[row * ROWS + i, panel] >> 8) > 1, i, at)
    return at


def pack(read, out_ref, code_ref, row, chip, panel):
    near = is_near(row, chip)

    @pl.when(near)
    def _():
        for i in range(ROWS):
            out_ref[i] = read(i)

    @pl.when(jnp.logical_not(near))
    def _():
        low = low_lanes()
        for g in range(2):
            for h in range(2):
                i = 4 * g + 2 * h
                out_ref[g, :, 128 * h : 128 * h + 128] = jnp.where(
                    low, read(i)[:, :128], turned(read(i + 1)[:, :128])
                )
        out_ref[2] = read(full_row(code_ref, row, panel))
        for i in range(SHORT, ROWS):
            out_ref[i] = jnp.zeros((BS, 256), F32)


def put(halves, hi_ref, lo_ref, at, i):
    rows = pl.ds(pl.multiple_of(i * BS, BS), BS)
    for t in range(2):
        hi = halves[t].astype(BF16)
        hi_ref[at, rows, 128 * t : 128 * t + 128] = hi
        lo_ref[at, rows, 128 * t : 128 * t + 128] = (halves[t] - hi.astype(F32)).astype(BF16)


def unpack(short_ref, short_at, rest_ref, rest_at, code_ref, row, panel, hi_ref, lo_ref, at):
    near = is_near(row, panel // 2)

    @pl.when(near)
    def _():
        @pl.loop(0, SHORT)
        def _(i):
            put(spread_row(short_ref[short_at + i], code_ref[row * ROWS + i, panel]), hi_ref, lo_ref, at, i)

        @pl.loop(SHORT, ROWS)
        def _(i):
            put(spread_row(rest_ref[rest_at + i - SHORT], code_ref[row * ROWS + i, panel]), hi_ref, lo_ref, at, i)

    @pl.when(jnp.logical_not(near))
    def _():
        low = low_lanes()
        for i in range(ROWS):
            code = code_ref[row * ROWS + i, panel]
            col, used = code & 3, (code >> 8) > 0
            h = (i % 4) // 2
            view = short_ref[short_at + i // 4, :, 128 * h : 128 * h + 128]
            other = turned(view)
            if i % 2 == 1:
                view, other = other, view
            halves = []
            for t in range(2):
                dense = jnp.where(lane_mask(low, (col == 2 * t) & used, jnp.bool_(False)), view, 0.0)
                dense = jnp.where(lane_mask(low, jnp.bool_(False), (col == 2 * t + 1) & used), other, dense)
                halves.append(dense)
            put(halves, hi_ref, lo_ref, at, i)
        full = full_row(code_ref, row, panel)
        put(spread_row(short_ref[short_at + 2], code_ref[row * ROWS + full, panel]), hi_ref, lo_ref, at, full)


def position():
    row = lax.axis_index("row")
    panel = lax.axis_index("col")
    return row, panel // 2, panel % 2, panel


def unpack_ring(parts, along_row, core, code_ref, hi_ref, lo_ref):
    row, chip, _, panel = position()
    place = chip if along_row else row
    half, spot = place // RING, place % RING
    for s, (short_ref, both_ref) in enumerate(parts):
        for flip in range(2):
            source = (half if flip == 0 else 1 - half) * RING + (spot - s + RING) % RING
            from_row, from_panel = (row, 2 * source + core) if along_row else (source, panel)
            unpack(
                short_ref if flip == 0 else both_ref,
                0,
                both_ref,
                SHORT,
                code_ref,
                from_row,
                from_panel,
                hi_ref,
                lo_ref,
                from_panel if along_row else from_row,
            )


def multiply(left_hi, left_lo, right_hi, right_lo, total):
    total[...] = jnp.zeros_like(total)

    @pl.loop(0, SIDES)
    def _(k):
        acc = total[...]
        for p in range(2):
            rows = pl.ds(256 * p, 256)
            a_hi, a_lo = left_hi[2 * k + p], left_lo[2 * k + p]
            b_hi, b_lo = right_hi[k, rows, :], right_lo[k, rows, :]
            acc += jnp.dot(a_hi, b_hi, preferred_element_type=F32)
            acc += jnp.dot(a_lo, b_hi, preferred_element_type=F32)
            acc += jnp.dot(a_hi, b_lo, preferred_element_type=F32)
        total[...] = acc


def pack_kernel(code_ref, matrix_ref, out_ref):
    row, chip, _, panel = position()
    pack(lambda i: matrix_ref[i], out_ref, code_ref, row, chip, panel)


def left_kernel(code_ref, *refs):
    mine = [(refs[2 * s], refs[2 * s + 1]) for s in range(RING)]
    others = [(refs[8 + 2 * s], refs[8 + 2 * s + 1]) for s in range(RING)]
    hi_ref, lo_ref = refs[16:]
    core = position()[2]
    unpack_ring(mine, True, core, code_ref, hi_ref, lo_ref)
    unpack_ring(others, True, 1 - core, code_ref, hi_ref, lo_ref)


def square_kernel(code_ref, left_hi, left_lo, *refs):
    parts = [(refs[2 * s], refs[2 * s + 1]) for s in range(RING)]
    out_ref, right_hi, right_lo, total, slots = refs[8:]
    row, chip, _, panel = position()
    unpack_ring(parts, False, None, code_ref, right_hi, right_lo)
    multiply(left_hi, left_lo, right_hi, right_lo, total)

    @pl.loop(0, ROWS)
    def _(i):
        tile = total[pl.ds(pl.multiple_of(i * BS, BS), BS), :]
        at_row = (row * ROWS + i) * BS + lax.broadcasted_iota(jnp.int32, (BS, 256), 0)
        at_col = panel * 256 + lax.broadcasted_iota(jnp.int32, (BS, 256), 1)
        tile = jnp.where(at_row == at_col, 3.0, 0.0) - tile
        first, second = collect_row(tile, code_ref[row * ROWS + i, panel])
        slots[i, :, :128] = first
        slots[i, :, 128:] = second

    pack(lambda i: slots[i], out_ref, code_ref, row, chip, panel)


def result_kernel(code_ref, left_hi, left_lo, *refs):
    parts = [(refs[2 * s], refs[2 * s + 1]) for s in range(RING)]
    out_ref, right_hi, right_lo, total = refs[8:]
    row, chip, _, panel = position()
    unpack_ring(parts, False, None, code_ref, right_hi, right_lo)
    multiply(left_hi, left_lo, right_hi, right_lo, total)

    @pl.loop(0, ROWS)
    def _(i):
        tile = 0.5 * total[pl.ds(pl.multiple_of(i * BS, BS), BS), :]
        first, second = collect_row(tile, code_ref[row * ROWS + i, panel])
        out_ref[i, :, :128] = first
        out_ref[i, :, 128:] = second


def call(kernel, inputs, outs, scratch=(), flops=0, nbytes=0):
    return pl.pallas_call(
        kernel,
        out_shape=outs,
        in_specs=[SMEM] + [VMEM] * (len(inputs) - 1),
        out_specs=jax.tree.map(lambda _: VMEM, outs),
        scratch_shapes=list(scratch),
        compiler_params=pltpu.CompilerParams(vmem_limit_bytes=48 * 2**20),
        cost_estimate=pl.CostEstimate(flops=flops, bytes_accessed=nbytes, transcendentals=0),
    )(*inputs)


def gather(packed, along_row, near):
    short, rest = packed[:SHORT], packed[SHORT:]
    flip_short = move(short, along_row, 1, 0)
    flip_rest = move(rest, along_row, 1, 0, near_only=True)
    shorts = [packed] + [move(short, along_row, 0, s) for s in (1, 2, 3)]
    both = jnp.concatenate([flip_short, jnp.where(near, rest, flip_rest)], axis=0)
    boths = [both] + [move(both, along_row, 0, s) for s in (1, 2, 3)]
    return [part for pair in zip(shorts, boths) for part in pair]


def per_device(matrix, pattern_cols, pattern_counts):
    row, panel = lax.axis_index("row"), lax.axis_index("col")
    near = is_near(row, panel // 2)
    weights = jnp.array([1, 4, 16, 64], jnp.int32)
    code = jnp.sum(pattern_cols * weights, axis=2) + pattern_counts * 256
    packed_shape = jax.ShapeDtypeStruct((ROWS, BS, 256), F32)
    packed = call(pack_kernel, [code, matrix], packed_shape)

    left = gather(packed, True, near)
    left = left + [other_core(part) for part in left]
    right = gather(packed, False, near)
    dense_shape = jax.ShapeDtypeStruct((2 * SIDES, ROWS * BS, 256), BF16)
    left_hi, left_lo = call(left_kernel, [code] + left, [dense_shape, dense_shape])

    right_scratch = [pltpu.VMEM((SIDES, ROWS * BS, 256), BF16)] * 2 + [pltpu.VMEM((ROWS * BS, 256), F32)]
    shifted = call(
        square_kernel,
        [code, left_hi, left_lo] + right,
        packed_shape,
        right_scratch + [pltpu.VMEM((ROWS, BS, 256), F32)],
    )
    right = gather(shifted, False, near)
    return call(result_kernel, [code, left_hi, left_lo] + right, packed_shape, right_scratch)


def solution(mesh):
    return jax.shard_map(
        per_device,
        mesh=mesh,
        in_specs=(P("row", None, "col"), P(), P()),
        out_specs=P("row", None, "col"),
        check_vma=False,
    )
```

```python
import jax
import jax.numpy as jnp
from jax import lax
from jax.experimental import pallas as pl
from jax.experimental.pallas import tpu as pltpu
from jax.sharding import PartitionSpec as P

ROWS = 8
HALF = ROWS // 2
BS = 64
RING = 4
SIDES = 8
VMEM = pl.BlockSpec(memory_space=pltpu.VMEM)
SMEM = pl.BlockSpec(memory_space=pltpu.SMEM)
BF16 = jnp.bfloat16
F32 = jnp.float32


def move(value, along_row, flip, shift):
    pairs = []
    for row in range(SIDES):
        for chip in range(SIDES):
            half, at = divmod(chip if along_row else row, RING)
            place = (half ^ flip) * RING + (at + shift) % RING
            target = (row, place) if along_row else (place, chip)
            for core in range(2):
                pairs.append(((row * SIDES + chip) * 2 + core, (target[0] * SIDES + target[1]) * 2 + core))
    return lax.ppermute(value, ("row", "col"), pairs)


def other_core(value):
    return lax.ppermute(value, "col", [(c, c ^ 1) for c in range(2 * SIDES)])


def gather_two_stages(value, along_row):
    one, three, two, across = [move(value, along_row, f, s) for f, s in ((0, 1), (0, 3), (0, 2), (1, 0))]
    near = [(value, 0, 0), (one, 0, 1), (three, 0, 3), (two, 0, 2)]
    far = [
        (across, 1, 0),
        (move(across, along_row, 0, 1), 1, 1),
        (move(across, along_row, 0, 3), 1, 3),
        (move(two, along_row, 1, 0), 1, 2),
    ]
    return [[([(a, 0, ROWS, 0)], f, s) for a, f, s in part] for part in (near, far)]


def gather_by_halves(value, along_row):
    across, one, three = [move(value, along_row, f, s) for f, s in ((1, 0), (0, 1), (0, 3))]
    low, high = move(one[:HALF], along_row, 0, 1), move(three[HALF:], along_row, 0, 3)
    near = [([(a, 0, ROWS, 0)], 0, s) for a, s in ((value, 0), (one, 1), (three, 3))]
    near.append(([(low, 0, HALF, 0), (high, 0, HALF, HALF)], 0, 2))
    far = [
        ([(a, 0, ROWS, 0)], 1, s)
        for a, s in ((across, 0), (move(across, along_row, 0, 1), 1), (move(across, along_row, 0, 3), 3))
    ]
    far.append(([(move(low, along_row, 1, 0), 0, HALF, 0), (move(high, along_row, 1, 0), 0, HALF, HALF)], 1, 2))
    return near, far


def turned(half):
    return pltpu.roll(half, BS, 1)


VIEWS = ((0, 1), (1, 0), (2, 3), (3, 2))


def views_of(tile):
    first, second = tile[:, :128], tile[:, 128:]
    return first, turned(first), second, turned(second)


def slot_cols(code):
    return [jnp.where((code >> 8) > a, (code >> (2 * a)) & 3, 7) for a in range(4)]


def spread_masks(code):
    cols = slot_cols(code)
    low = lax.broadcasted_iota(jnp.int32, (16, 128), 1) < BS
    high = jnp.where(low, 0, 1)
    found = [jnp.where(low, cols[a], cols[b]) for a, b in VIEWS]
    return [[f == high + 2 * t for f in found] for t in range(2)]


def collect_masks(code):
    cols = slot_cols(code)
    low = lax.broadcasted_iota(jnp.int32, (16, 128), 1) < BS
    wanted = [jnp.where(low, cols[2 * u], cols[2 * u + 1]) for u in range(2)]
    return [[w == jnp.where(low, j, k) for j, k in VIEWS] for w in wanted]


def choose(masks, views):
    out = jnp.zeros((16, 128), F32)
    for mask, view in zip(masks, views):
        out = jnp.where(mask, view, out)
    return out


def position():
    panel = lax.axis_index("col")
    return lax.axis_index("row"), panel // 2, panel % 2


def put(tile, masks, hi_ref, lo_ref, at, first_row, first_col):
    for g in range(BS // 16):
        rows = slice(first_row + 16 * g, first_row + 16 * g + 16)
        views = views_of(tile[16 * g : 16 * g + 16, :])
        for t in range(2):
            cols = slice(first_col + 128 * t, first_col + 128 * t + 128)
            dense = choose(masks[t], views)
            hi = dense.astype(BF16)
            hi_ref[at, rows, cols] = hi
            lo_ref[at, rows, cols] = (dense - hi.astype(F32)).astype(BF16)


def source_of(place, flip, shift):
    half, spot = place // RING, place % RING
    return (half if flip == 0 else 1 - half) * RING + (spot - shift + RING) % RING


def unpack_left(shards, refs, code_ref, hi_ref, lo_ref):
    row, chip, core = position()
    for pieces, flip, shift in shards:
        source = source_of(chip, flip, shift)
        for at, first, count, start in pieces:
            for n in range(count):
                i = start + n
                masks = spread_masks(code_ref[row * ROWS + i, 2 * source + core])
                put(refs[at][first + n], masks, hi_ref, lo_ref, source, BS * i, 0)


def unpack_right(shards, refs, code_ref, hi_ref, lo_ref):
    row, chip, core = position()
    for pieces, flip, shift in shards:
        source = source_of(row, flip, shift)
        for at, first, count, start in pieces:
            for n in range(count):
                part, i = divmod(start + n, HALF)
                panel = 2 * chip + (core if part == 0 else 1 - core)
                masks = spread_masks(code_ref[source * ROWS + HALF * core + i, panel])
                put(refs[at][first + n], masks, hi_ref, lo_ref, source, BS * i, 256 * part)


def multiply(left_hi, left_lo, right_hi, right_lo, total):
    lefts, rights = [], []
    for k in range(SIDES):
        lefts += [left_hi[k], left_lo[k], left_hi[k]]
        rights += [right_hi[k], right_hi[k], right_lo[k]]
    total[...] = jnp.dot(
        jnp.concatenate(lefts, axis=1), jnp.concatenate(rights, axis=0), preferred_element_type=F32
    )


def flatten(shards):
    arrays, placed = [], []
    for pieces, flip, shift in shards:
        placed.append(([(len(arrays) + n, *piece[1:]) for n, piece in enumerate(pieces)], flip, shift))
        arrays += [piece[0] for piece in pieces]
    return arrays, placed


ANYWHERE = pl.BlockSpec(memory_space=pl.ANY)
LEFT = jax.ShapeDtypeStruct((SIDES, ROWS * BS, 256), BF16)
RIGHT = jax.ShapeDtypeStruct((SIDES, HALF * BS, 512), BF16)
SLOTS = jax.ShapeDtypeStruct((ROWS, BS, 256), F32)


def product(code, left_shards, left_dense, right_shards, last):
    left_arrays, left_plan = flatten(left_shards)
    right_arrays, right_plan = flatten(right_shards)
    n_left, n_right = len(left_arrays), len(right_arrays)

    def kernel(code_ref, *refs):
        left_refs, refs = refs[:n_left], refs[n_left:]
        right_refs, refs = refs[:n_right], refs[n_right:]
        if last:
            hbm, (mine_ref, other_ref), refs = refs[:2], refs[2:4], refs[4:]
        else:
            (mine_ref, other_ref), hbm, refs = refs[:2], refs[2:4], refs[4:]
        left_hi, left_lo, right_hi, right_lo, total, sems = refs
        row, chip, core = position()
        moves = []
        for n, (far, here) in enumerate(zip(hbm, (left_hi, left_lo))):
            ends = (far, here) if last else (here, far)
            moves.append(pltpu.make_async_copy(*ends, sems.at[n]))
        unpack_left(left_plan, left_refs, code_ref, left_hi, left_lo)
        for m in moves:
            m.start()
        unpack_right(right_plan, right_refs, code_ref, right_hi, right_lo)
        if last:
            for m in moves:
                m.wait()
        multiply(left_hi, left_lo, right_hi, right_lo, total)

        for part in range(2):
            panel = 2 * chip + (core if part == 0 else 1 - core)
            for n in range(ROWS):
                if last:
                    i, out_ref, at = n, (mine_ref, other_ref)[part], n
                elif n < HALF:
                    i, out_ref, at = HALF * core + n, mine_ref, HALF * part + n
                else:
                    i, out_ref, at = HALF * (1 - core) + n - HALF, other_ref, HALF * (1 - part) + n - HALF
                masks = collect_masks(code_ref[row * ROWS + i, panel])
                for g in range(BS // 16):
                    first = i * BS + 16 * g
                    rows = pl.ds(first if last else pl.multiple_of(first, 16), 16)
                    tile = total[rows, 256 * part : 256 * part + 256]
                    if last:
                        tile = 0.5 * tile
                    elif n < HALF:
                        at_row = row * ROWS * BS + first + lax.broadcasted_iota(jnp.int32, (16, 256), 0)
                        at_col = panel * 256 + lax.broadcasted_iota(jnp.int32, (16, 256), 1)
                        tile = jnp.where(at_row == at_col, 3.0, 0.0) - tile
                    else:
                        tile = -tile
                    views = views_of(tile)
                    for u in range(2):
                        out_ref[at, 16 * g : 16 * g + 16, 128 * u : 128 * u + 128] = choose(masks[u], views)

        if not last:
            for m in moves:
                m.wait()

    return pl.pallas_call(
        kernel,
        out_shape=[SLOTS, SLOTS] if last else [SLOTS, SLOTS, LEFT, LEFT],
        in_specs=[SMEM] + [VMEM] * (n_left + n_right) + [ANYWHERE] * len(left_dense),
        out_specs=[VMEM, VMEM] if last else [VMEM, VMEM, ANYWHERE, ANYWHERE],
        scratch_shapes=[
            *[pltpu.VMEM(LEFT.shape, BF16)] * 2,
            *[pltpu.VMEM(RIGHT.shape, BF16)] * 2,
            pltpu.VMEM((ROWS * BS, 512), F32),
            pltpu.SemaphoreType.DMA((2,)),
        ],
        compiler_params=pltpu.CompilerParams(vmem_limit_bytes=20 * 2**20),
        cost_estimate=pl.CostEstimate(flops=3 * 2**30, bytes_accessed=2**24, transcendentals=0),
    )(code, *left_arrays, *right_arrays, *left_dense)


def per_device(matrix, pattern_cols, pattern_counts):
    weights = jnp.array([1, 4, 16, 64], jnp.int32)
    code = jnp.sum(pattern_cols * weights, axis=2) + pattern_counts * 256
    core = lax.axis_index("col") % 2

    keep = lax.dynamic_slice_in_dim(matrix, HALF * core, HALF, 0)
    send = lax.dynamic_slice_in_dim(matrix, HALF * (1 - core), HALF, 0)
    halves = jnp.concatenate([keep, other_core(send)], axis=0)
    left = sum(gather_two_stages(matrix, True), [])
    right = sum(gather_two_stages(halves, False), [])
    mine, other, *left = product(code, left, [], right, False)

    right = sum(gather_by_halves(mine + other_core(other), False), [])
    mine, other = product(code, [], left, right, True)
    return mine + other_core(other)


def solution(mesh):
    return jax.shard_map(
        per_device,
        mesh=mesh,
        in_specs=(P("row", None, "col"), P(), P()),
        out_specs=P("row", None, "col"),
        check_vma=False,
    )
```

```python
import jax
import jax.numpy as jnp
from jax import lax
from jax.experimental import pallas as pl
from jax.experimental.pallas import tpu as pltpu
from jax.sharding import PartitionSpec as P

ROWS = 8
HALF = ROWS // 2
BS = 64
RING = 4
KINDS = ("M", "M", "M")
TIE = False
SIDES = 8
VMEM = pl.BlockSpec(memory_space=pltpu.VMEM)
SMEM = pl.BlockSpec(memory_space=pltpu.SMEM)
BF16 = jnp.bfloat16
F32 = jnp.float32


def move(value, along_row, flip, shift):
    pairs = []
    for row in range(SIDES):
        for chip in range(SIDES):
            half, at = divmod(chip if along_row else row, RING)
            place = (half ^ flip) * RING + (at + shift) % RING
            target = (row, place) if along_row else (place, chip)
            for core in range(2):
                pairs.append(((row * SIDES + chip) * 2 + core, (target[0] * SIDES + target[1]) * 2 + core))
    return lax.ppermute(value, ("row", "col"), pairs)


def other_core(value):
    return lax.ppermute(value, "col", [(c, c ^ 1) for c in range(2 * SIDES)])


def whole(array, flip, shift):
    return [(array, 0, ROWS, 0)], flip, shift


def by_half(low, high, flip, first=(0, 0)):
    return [(low, first[0], HALF, 0), (high, first[1], HALF, HALF)], flip, 2


def gather(value, along_row, kind, use_early=None):
    step = lambda v, flip, shift: move(v, along_row, flip, shift)
    across, one, three = step(value, 1, 0), step(value, 0, 1), step(value, 0, 3)
    low = high = two = None
    if kind in ("P", "L7", "L8"):
        two = step(value, 0, 2)
        own_two = whole(two, 0, 2)
    elif kind == "W":
        two = step(one, 0, 1)
        own_two = whole(two, 0, 2)
    else:
        low, high = step(one[:HALF], 0, 1), step(three[HALF:], 0, 3)
        own_two = by_half(low, high, 0)
    early = [whole(value, 0, 0), whole(one, 0, 1), whole(three, 0, 3), own_two, whole(across, 1, 0)]
    used = None
    if use_early:
        used = list(use_early(early))
        if TIE and two is not None and kind in ("P", "W"):
            two, used[0] = lax.optimization_barrier((two, used[0]))
    g1, g3 = step(across, 0, 1), step(across, 0, 3)
    if kind in ("P", "W"):
        far_two = whole(step(two, 1, 0), 1, 2)
    elif kind == "F":
        far_two = by_half(step(low, 1, 0), step(high, 1, 0), 1)
    elif kind == "M":
        both = step(jnp.concatenate([low, high], axis=0), 1, 0)
        far_two = whole(both, 1, 2)
    elif kind == "L7":
        far_two = whole(step(g1, 0, 1), 1, 2)
    else:
        far_two = by_half(step(g1[:HALF], 0, 1), step(g3[HALF:], 0, 3), 1)
    late = [whole(g1, 1, 1), whole(g3, 1, 3), far_two]
    return early, used, late


def turned(half):
    return pltpu.roll(half, BS, 1)


VIEWS = ((0, 1), (1, 0), (2, 3), (3, 2))


def views_of(tile):
    first, second = tile[:, :128], tile[:, 128:]
    return first, turned(first), second, turned(second)


def slot_cols(code):
    return [jnp.where((code >> 8) > a, (code >> (2 * a)) & 3, 7) for a in range(4)]


def spread_masks(code):
    cols = slot_cols(code)
    low = lax.broadcasted_iota(jnp.int32, (16, 128), 1) < BS
    high = jnp.where(low, 0, 1)
    found = [jnp.where(low, cols[a], cols[b]) for a, b in VIEWS]
    return [[f == high + 2 * t for f in found] for t in range(2)]


def collect_masks(code):
    cols = slot_cols(code)
    low = lax.broadcasted_iota(jnp.int32, (16, 128), 1) < BS
    wanted = [jnp.where(low, cols[2 * u], cols[2 * u + 1]) for u in range(2)]
    return [[w == jnp.where(low, j, k) for j, k in VIEWS] for w in wanted]


def choose(masks, views):
    out = jnp.zeros((16, 128), F32)
    for mask, view in zip(masks, views):
        out = jnp.where(mask, view, out)
    return out


def position():
    panel = lax.axis_index("col")
    return lax.axis_index("row"), panel // 2, panel % 2


def put(tile, masks, hi_ref, lo_ref, at, first_row, first_col):
    for g in range(BS // 16):
        rows = slice(first_row + 16 * g, first_row + 16 * g + 16)
        views = views_of(tile[16 * g : 16 * g + 16, :])
        for t in range(2):
            cols = slice(first_col + 128 * t, first_col + 128 * t + 128)
            dense = choose(masks[t], views)
            hi = dense.astype(BF16)
            hi_ref[at, rows, cols] = hi
            lo_ref[at, rows, cols] = (dense - hi.astype(F32)).astype(BF16)


def source_of(place, flip, shift):
    half, spot = place // RING, place % RING
    return (half if flip == 0 else 1 - half) * RING + (spot - shift + RING) % RING


def unpack_left(shards, refs, code_ref, hi_ref, lo_ref, by_source):
    row, chip, core = position()
    for place, (pieces, flip, shift) in enumerate(shards):
        source = source_of(chip, flip, shift)
        for at, first, count, start in pieces:
            for n in range(count):
                i = start + n
                masks = spread_masks(code_ref[row * ROWS + i, 2 * source + core])
                put(refs[at][first + n], masks, hi_ref, lo_ref, source if by_source else place, BS * i, 0)


def unpack_right(shards, refs, code_ref, hi_ref, lo_ref, by_source):
    row, chip, core = position()
    for place, (pieces, flip, shift) in enumerate(shards):
        source = source_of(row, flip, shift)
        for at, first, count, start in pieces:
            for n in range(count):
                part, i = divmod(start + n, HALF)
                panel = 2 * chip + (core if part == 0 else 1 - core)
                masks = spread_masks(code_ref[source * ROWS + HALF * core + i, panel])
                at_place = source if by_source else place
                put(refs[at][first + n], masks, hi_ref, lo_ref, at_place, BS * i, 256 * part)


def multiply(left_hi, left_lo, right_hi, right_lo, count):
    lefts, rights = [], []
    for k in range(count):
        lefts += [left_hi[k], left_lo[k], left_hi[k]]
        rights += [right_hi[k], right_hi[k], right_lo[k]]
    return jnp.dot(jnp.concatenate(lefts, axis=1), jnp.concatenate(rights, axis=0), preferred_element_type=F32)


def collect(total, code_ref, part, i, finish, out_ref, at):
    row, chip, core = position()
    panel = 2 * chip + (core if part == 0 else 1 - core)
    masks = collect_masks(code_ref[row * ROWS + i, panel])
    for g in range(BS // 16):
        first = i * BS + 16 * g
        rows = pl.ds(first if isinstance(first, int) else pl.multiple_of(first, 16), 16)
        views = views_of(finish(total[rows, 256 * part : 256 * part + 256], row * ROWS * BS + first, panel * 256))
        for u in range(2):
            out_ref[at, 16 * g : 16 * g + 16, 128 * u : 128 * u + 128] = choose(masks[u], views)


def from_three(tile, first_row, first_col):
    at_row = first_row + lax.broadcasted_iota(jnp.int32, (16, 256), 0)
    at_col = first_col + lax.broadcasted_iota(jnp.int32, (16, 256), 1)
    return jnp.where(at_row == at_col, 3.0, 0.0) - tile


def flatten(shards):
    arrays, placed = [], []
    for pieces, flip, shift in shards:
        placed.append(([(len(arrays) + n, *piece[1:]) for n, piece in enumerate(pieces)], flip, shift))
        arrays += [piece[0] for piece in pieces]
    return arrays, placed


ANYWHERE = pl.BlockSpec(memory_space=pl.ANY)
SLOTS = jax.ShapeDtypeStruct((ROWS, BS, 256), F32)


def left_shape(count):
    return (count, ROWS * BS, 256)


def right_shape(count):
    return (count, HALF * BS, 512)


def call(kernel, inputs, in_specs, outs, out_specs, scratch, megabytes, microseconds):
    return pl.pallas_call(
        kernel,
        out_shape=outs,
        in_specs=in_specs,
        out_specs=out_specs,
        scratch_shapes=scratch,
        compiler_params=pltpu.CompilerParams(vmem_limit_bytes=megabytes * 2**20),
        cost_estimate=pl.CostEstimate(flops=0, bytes_accessed=microseconds * 3_000_000, transcendentals=0),
    )(*inputs)


def make_dense(code, along_row, shards):
    arrays, plan = flatten(shards)
    unpack, shape = (unpack_left, left_shape) if along_row else (unpack_right, right_shape)

    def kernel(code_ref, *refs):
        unpack(plan, refs, code_ref, refs[-2], refs[-1], False)

    outs = [jax.ShapeDtypeStruct(shape(len(shards)), BF16)] * 2
    return call(kernel, [code, *arrays], [SMEM] + [VMEM] * len(arrays), outs, [VMEM] * 2, [], 8, 2)


def square(code, early, dense, left_shards, right_shards):
    left_arrays, left_plan = flatten(left_shards)
    right_arrays, right_plan = flatten(right_shards)
    n_left = len(left_arrays)
    n_in = n_left + len(right_arrays)
    places = [(flip, shift) for _, flip, shift in early]

    def kernel(code_ref, *refs):
        near, refs = refs[:4], refs[4:]
        left_refs, right_refs, refs = refs[:n_left], refs[n_left:n_in], refs[n_in:]
        keep_ref, send_ref, *stored = refs[:4]
        *sides, total, load_sems, store_sems = refs[4:]
        row, chip, core = position()
        loads = []
        for n, (there, here) in enumerate(zip(near, sides)):
            for k, (flip, shift) in enumerate(places):
                at = here.at[source_of(chip if n < 2 else row, flip, shift)]
                loads.append(pltpu.make_async_copy(there.at[k], at, load_sems.at[n * len(places) + k]))
        for m in loads:
            m.start()
        unpack_left(left_plan, left_refs, code_ref, sides[0], sides[1], True)
        unpack_right(right_plan, right_refs, code_ref, sides[2], sides[3], True)
        for m in loads:
            m.wait()
        stores = [pltpu.make_async_copy(sides[n], stored[n], store_sems.at[n]) for n in range(2)]
        for m in stores:
            m.start()
        total[...] = multiply(*sides, SIDES)
        for part in range(2):
            for n in range(HALF):
                collect(total, code_ref, part, HALF * core + n, from_three, keep_ref, HALF * part + n)
                collect(
                    total, code_ref, part, HALF * (1 - core) + n, lambda t, *_: -t, send_ref, HALF * (1 - part) + n
                )
        for m in stores:
            m.wait()

    left = jax.ShapeDtypeStruct(left_shape(SIDES), BF16)
    return call(
        kernel,
        [code, *dense, *left_arrays, *right_arrays],
        [SMEM] + [ANYWHERE] * 4 + [VMEM] * n_in,
        [SLOTS, SLOTS, left, left],
        [VMEM, VMEM, ANYWHERE, ANYWHERE],
        [
            *[pltpu.VMEM(left_shape(SIDES), BF16)] * 2,
            *[pltpu.VMEM(right_shape(SIDES), BF16)] * 2,
            pltpu.VMEM((ROWS * BS, 512), F32),
            pltpu.SemaphoreType.DMA((4 * len(places),)),
            pltpu.SemaphoreType.DMA((2,)),
        ],
        20,
        9,
    )


def times(code, left, right_shards, before=None):
    arrays, plan = flatten(right_shards)
    n_in, count = len(arrays), len(right_shards)
    extra = [] if before is None else [before]

    def kernel(code_ref, far_hi, far_lo, *refs):
        arrived, refs = refs[:n_in], refs[n_in:]
        before_ref, refs = refs[: len(extra)], refs[len(extra) :]
        outs, refs = refs[: 1 + len(extra)], refs[1 + len(extra) :]
        *sides, sems = refs
        row, _, _ = position()
        loads = []
        for k, (_, flip, shift) in enumerate(plan):
            source = source_of(row, flip, shift)
            for n, far in enumerate((far_hi, far_lo)):
                loads.append(pltpu.make_async_copy(far.at[source], sides[n].at[k], sems.at[2 * k + n]))
        for m in loads:
            m.start()
        unpack_right(plan, arrived, code_ref, sides[2], sides[3], False)
        for m in loads:
            m.wait()
        if not extra:
            outs[0][...] = multiply(*sides[:4], count)
            return
        total = sides[4]
        total[...] = before_ref[0][...] + multiply(*sides[:4], count)
        for part in range(2):
            for i in range(ROWS):
                collect(total, code_ref, part, i, lambda t, *_: 0.5 * t, outs[part], i)

    dense = jax.ShapeDtypeStruct((ROWS * BS, 512), F32)
    return call(
        kernel,
        [code, *left, *arrays, *extra],
        [SMEM] + [ANYWHERE] * 2 + [VMEM] * (n_in + len(extra)),
        [SLOTS, SLOTS] if extra else [dense],
        [VMEM, VMEM] if extra else [VMEM],
        [
            *[pltpu.VMEM(left_shape(count), BF16)] * 2,
            *[pltpu.VMEM(right_shape(count), BF16)] * 2,
            *([pltpu.VMEM((ROWS * BS, 512), F32)] if extra else []),
            pltpu.SemaphoreType.DMA((2 * count,)),
        ],
        14,
        4,
    )


def per_device(matrix, pattern_cols, pattern_counts):
    weights = jnp.array([1, 4, 16, 64], jnp.int32)
    code = jnp.sum(pattern_cols * weights, axis=2) + pattern_counts * 256
    core = lax.axis_index("col") % 2

    keep = lax.dynamic_slice_in_dim(matrix, HALF * core, HALF, 0)
    send = lax.dynamic_slice_in_dim(matrix, HALF * (1 - core), HALF, 0)
    halves = jnp.concatenate([keep, other_core(send)], axis=0)
    left_early, left_dense, left_late = gather(matrix, True, KINDS[0], lambda x: make_dense(code, True, x))
    right_early, right_dense, right_late = gather(halves, False, KINDS[1], lambda x: make_dense(code, False, x))
    keep, send, *left = square(code, left_early, left_dense + right_dense, left_late, right_late)

    early, _, late = gather(keep + other_core(send), False, KINDS[2])
    part = times(code, left, early)[0]
    mine, other = times(code, left, late, part)
    return mine + other_core(other)


def solution(mesh):
    return jax.shard_map(
        per_device,
        mesh=mesh,
        in_specs=(P("row", None, "col"), P(), P()),
        out_specs=P("row", None, "col"),
        check_vma=False,
    )
```

```python
import jax
import jax.numpy as jnp
from jax import lax
from jax.experimental import pallas as pl
from jax.experimental.pallas import tpu as pltpu
from jax.sharding import PartitionSpec as P

ROWS = 8
HALF = ROWS // 2
BS = 64
RING = 4
KINDS = ("M", "M", "F")
TIE = False
SIDES = 8
VMEM = pl.BlockSpec(memory_space=pltpu.VMEM)
SMEM = pl.BlockSpec(memory_space=pltpu.SMEM)
BF16 = jnp.bfloat16
F32 = jnp.float32


def move(value, along_row, flip, shift):
    pairs = []
    for row in range(SIDES):
        for chip in range(SIDES):
            half, at = divmod(chip if along_row else row, RING)
            place = (half ^ flip) * RING + (at + shift) % RING
            target = (row, place) if along_row else (place, chip)
            for core in range(2):
                pairs.append(((row * SIDES + chip) * 2 + core, (target[0] * SIDES + target[1]) * 2 + core))
    return lax.ppermute(value, ("row", "col"), pairs)


def other_core(value):
    return lax.ppermute(value, "col", [(c, c ^ 1) for c in range(2 * SIDES)])


def whole(array, flip, shift):
    return [(array, 0, ROWS, 0)], flip, shift


def by_half(low, high, flip, first=(0, 0)):
    return [(low, first[0], HALF, 0), (high, first[1], HALF, HALF)], flip, 2


def gather(value, along_row, kind, use_early=None):
    step = lambda v, flip, shift: move(v, along_row, flip, shift)
    across, one, three = step(value, 1, 0), step(value, 0, 1), step(value, 0, 3)
    low = high = two = None
    if kind in ("P", "L7", "L8"):
        two = step(value, 0, 2)
        own_two = whole(two, 0, 2)
    elif kind == "W":
        two = step(one, 0, 1)
        own_two = whole(two, 0, 2)
    else:
        low, high = step(one[:HALF], 0, 1), step(three[HALF:], 0, 3)
        own_two = by_half(low, high, 0)
    early = [whole(value, 0, 0), whole(one, 0, 1), whole(three, 0, 3), own_two, whole(across, 1, 0)]
    used = None
    if use_early:
        used = list(use_early(early))
        if TIE and two is not None and kind in ("P", "W"):
            two, used[0] = lax.optimization_barrier((two, used[0]))
    g1, g3 = step(across, 0, 1), step(across, 0, 3)
    if kind in ("P", "W"):
        far_two = whole(step(two, 1, 0), 1, 2)
    elif kind == "F":
        far_two = by_half(step(low, 1, 0), step(high, 1, 0), 1)
    elif kind == "M":
        both = step(jnp.concatenate([low, high], axis=0), 1, 0)
        far_two = whole(both, 1, 2)
    elif kind == "L7":
        far_two = whole(step(g1, 0, 1), 1, 2)
    else:
        far_two = by_half(step(g1[:HALF], 0, 1), step(g3[HALF:], 0, 3), 1)
    late = [whole(g1, 1, 1), whole(g3, 1, 3), far_two]
    return early, used, late


def turned(half):
    return pltpu.roll(half, BS, 1)


VIEWS = ((0, 1), (1, 0), (2, 3), (3, 2))


def views_of(tile):
    first, second = tile[:, :128], tile[:, 128:]
    return first, turned(first), second, turned(second)


def slot_cols(code):
    return [jnp.where((code >> 8) > a, (code >> (2 * a)) & 3, 7) for a in range(4)]


def spread_masks(code):
    cols = slot_cols(code)
    low = lax.broadcasted_iota(jnp.int32, (16, 128), 1) < BS
    high = jnp.where(low, 0, 1)
    found = [jnp.where(low, cols[a], cols[b]) for a, b in VIEWS]
    return [[f == high + 2 * t for f in found] for t in range(2)]


def collect_masks(code):
    cols = slot_cols(code)
    low = lax.broadcasted_iota(jnp.int32, (16, 128), 1) < BS
    wanted = [jnp.where(low, cols[2 * u], cols[2 * u + 1]) for u in range(2)]
    return [[w == jnp.where(low, j, k) for j, k in VIEWS] for w in wanted]


def choose(masks, views):
    out = jnp.zeros((16, 128), F32)
    for mask, view in zip(masks, views):
        out = jnp.where(mask, view, out)
    return out


def position():
    panel = lax.axis_index("col")
    return lax.axis_index("row"), panel // 2, panel % 2


def put(tile, masks, hi_ref, lo_ref, at, first_row, first_col):
    for g in range(BS // 16):
        rows = slice(first_row + 16 * g, first_row + 16 * g + 16)
        views = views_of(tile[16 * g : 16 * g + 16, :])
        for t in range(2):
            cols = slice(first_col + 128 * t, first_col + 128 * t + 128)
            dense = choose(masks[t], views)
            hi = dense.astype(BF16)
            hi_ref[at, rows, cols] = hi
            lo_ref[at, rows, cols] = (dense - hi.astype(F32)).astype(BF16)


def source_of(place, flip, shift):
    half, spot = place // RING, place % RING
    return (half if flip == 0 else 1 - half) * RING + (spot - shift + RING) % RING


def unpack_left(shards, refs, code_ref, hi_ref, lo_ref, by_source):
    row, chip, core = position()
    for place, (pieces, flip, shift) in enumerate(shards):
        source = source_of(chip, flip, shift)
        for at, first, count, start in pieces:
            for n in range(count):
                i = start + n
                masks = spread_masks(code_ref[row * ROWS + i, 2 * source + core])
                put(refs[at][first + n], masks, hi_ref, lo_ref, source if by_source else place, BS * i, 0)


def unpack_right(shards, refs, code_ref, hi_ref, lo_ref, by_source):
    row, chip, core = position()
    for place, (pieces, flip, shift) in enumerate(shards):
        source = source_of(row, flip, shift)
        for at, first, count, start in pieces:
            for n in range(count):
                part, i = divmod(start + n, HALF)
                panel = 2 * chip + (core if part == 0 else 1 - core)
                masks = spread_masks(code_ref[source * ROWS + HALF * core + i, panel])
                at_place = source if by_source else place
                put(refs[at][first + n], masks, hi_ref, lo_ref, at_place, BS * i, 256 * part)


def multiply(left_hi, left_lo, right_hi, right_lo, count):
    lefts, rights = [], []
    for k in range(count):
        lefts += [left_hi[k], left_lo[k], left_hi[k]]
        rights += [right_hi[k], right_hi[k], right_lo[k]]
    return jnp.dot(jnp.concatenate(lefts, axis=1), jnp.concatenate(rights, axis=0), preferred_element_type=F32)


def collect(total, code_ref, part, i, finish, out_ref, at):
    row, chip, core = position()
    panel = 2 * chip + (core if part == 0 else 1 - core)
    masks = collect_masks(code_ref[row * ROWS + i, panel])
    for g in range(BS // 16):
        first = i * BS + 16 * g
        rows = pl.ds(first if isinstance(first, int) else pl.multiple_of(first, 16), 16)
        views = views_of(finish(total[rows, 256 * part : 256 * part + 256], row * ROWS * BS + first, panel * 256))
        for u in range(2):
            out_ref[at, 16 * g : 16 * g + 16, 128 * u : 128 * u + 128] = choose(masks[u], views)


def from_three(tile, first_row, first_col):
    at_row = first_row + lax.broadcasted_iota(jnp.int32, (16, 256), 0)
    at_col = first_col + lax.broadcasted_iota(jnp.int32, (16, 256), 1)
    return jnp.where(at_row == at_col, 3.0, 0.0) - tile


def flatten(shards):
    arrays, placed = [], []
    for pieces, flip, shift in shards:
        placed.append(([(len(arrays) + n, *piece[1:]) for n, piece in enumerate(pieces)], flip, shift))
        arrays += [piece[0] for piece in pieces]
    return arrays, placed


ANYWHERE = pl.BlockSpec(memory_space=pl.ANY)
SLOTS = jax.ShapeDtypeStruct((ROWS, BS, 256), F32)


def left_shape(count):
    return (count, ROWS * BS, 256)


def right_shape(count):
    return (count, HALF * BS, 512)


def call(kernel, inputs, in_specs, outs, out_specs, scratch, megabytes, microseconds):
    return pl.pallas_call(
        kernel,
        out_shape=outs,
        in_specs=in_specs,
        out_specs=out_specs,
        scratch_shapes=scratch,
        compiler_params=pltpu.CompilerParams(vmem_limit_bytes=megabytes * 2**20),
        cost_estimate=pl.CostEstimate(flops=0, bytes_accessed=microseconds * 3_000_000, transcendentals=0),
    )(*inputs)


def make_dense(code, along_row, shards):
    arrays, plan = flatten(shards)
    unpack, shape = (unpack_left, left_shape) if along_row else (unpack_right, right_shape)

    def kernel(code_ref, *refs):
        unpack(plan, refs, code_ref, refs[-2], refs[-1], False)

    outs = [jax.ShapeDtypeStruct(shape(len(shards)), BF16)] * 2
    return call(kernel, [code, *arrays], [SMEM] + [VMEM] * len(arrays), outs, [VMEM] * 2, [], 8, 2)


def square(code, left_shards, left_dense, right_early, right_dense, right_shards):
    right_arrays, right_plan = flatten(right_shards)
    n_left, n_right = 2 * len(left_dense), len(right_arrays)
    places = [(n, k, flip, shift) for n, part in enumerate(left_shards) for k, (_, flip, shift) in enumerate(part)]

    def kernel(code_ref, *refs):
        lefts, refs = refs[:n_left], refs[n_left:]
        early, refs = refs[:2], refs[2:]
        right_refs, refs = refs[:n_right], refs[n_right:]
        keep_ref, send_ref, *stored = refs[:4]
        right_hi, right_lo, total, load_sems, store_sems = refs[4:]
        row, chip, core = position()
        loads = []
        for k, (_, flip, shift) in enumerate(right_early):
            source = source_of(row, flip, shift)
            for m, here in enumerate((right_hi, right_lo)):
                loads.append(pltpu.make_async_copy(early[m].at[k], here.at[source], load_sems.at[2 * k + m]))
        pairs, stores = [], []
        for at, (n, k, flip, shift) in enumerate(places):
            source = source_of(chip, flip, shift)
            pairs.append((lefts[2 * n], lefts[2 * n + 1], k, source))
            for m in range(2):
                there = stored[m].at[source]
                stores.append(pltpu.make_async_copy(lefts[2 * n + m].at[k], there, store_sems.at[2 * at + m]))
        for m in loads + stores:
            m.start()
        unpack_right(right_plan, right_refs, code_ref, right_hi, right_lo, True)
        for m in loads:
            m.wait()
        ones, others = [], []
        for left_hi, left_lo, k, source in pairs:
            ones += [left_hi[k], left_lo[k], left_hi[k]]
            others += [right_hi[source], right_hi[source], right_lo[source]]
        total[...] = jnp.dot(
            jnp.concatenate(ones, axis=1), jnp.concatenate(others, axis=0), preferred_element_type=F32
        )
        for part in range(2):
            for n in range(HALF):
                collect(total, code_ref, part, HALF * core + n, from_three, keep_ref, HALF * part + n)
                collect(
                    total, code_ref, part, HALF * (1 - core) + n, lambda t, *_: -t, send_ref, HALF * (1 - part) + n
                )
        for m in stores:
            m.wait()

    left = jax.ShapeDtypeStruct(left_shape(SIDES), BF16)
    return call(
        kernel,
        [code, *[a for pair in left_dense for a in pair], *right_dense, *right_arrays],
        [SMEM] + [VMEM] * (n_left + 2 + n_right),
        [SLOTS, SLOTS, left, left],
        [VMEM, VMEM, ANYWHERE, ANYWHERE],
        [
            *[pltpu.VMEM(right_shape(SIDES), BF16)] * 2,
            pltpu.VMEM((ROWS * BS, 512), F32),
            pltpu.SemaphoreType.DMA((2 * len(right_early),)),
            pltpu.SemaphoreType.DMA((2 * len(places),)),
        ],
        20,
        8,
    )


def times(code, left, right_shards, before=None):
    arrays, plan = flatten(right_shards)
    n_in, count = len(arrays), len(right_shards)
    extra = [] if before is None else [before]

    def kernel(code_ref, far_hi, far_lo, *refs):
        arrived, refs = refs[:n_in], refs[n_in:]
        before_ref, refs = refs[: len(extra)], refs[len(extra) :]
        outs, refs = refs[: 1 + len(extra)], refs[1 + len(extra) :]
        *sides, sems = refs
        row, _, _ = position()
        loads = []
        for k, (_, flip, shift) in enumerate(plan):
            source = source_of(row, flip, shift)
            for n, far in enumerate((far_hi, far_lo)):
                loads.append(pltpu.make_async_copy(far.at[source], sides[n].at[k], sems.at[2 * k + n]))
        for m in loads:
            m.start()
        unpack_right(plan, arrived, code_ref, sides[2], sides[3], False)
        for m in loads:
            m.wait()
        if not extra:
            outs[0][...] = multiply(*sides[:4], count)
            return
        total = sides[4]
        total[...] = before_ref[0][...] + multiply(*sides[:4], count)
        for part in range(2):
            for i in range(ROWS):
                collect(total, code_ref, part, i, lambda t, *_: 0.5 * t, outs[part], i)

    dense = jax.ShapeDtypeStruct((ROWS * BS, 512), F32)
    return call(
        kernel,
        [code, *left, *arrays, *extra],
        [SMEM] + [ANYWHERE] * 2 + [VMEM] * (n_in + len(extra)),
        [SLOTS, SLOTS] if extra else [dense],
        [VMEM, VMEM] if extra else [VMEM],
        [
            *[pltpu.VMEM(left_shape(count), BF16)] * 2,
            *[pltpu.VMEM(right_shape(count), BF16)] * 2,
            *([pltpu.VMEM((ROWS * BS, 512), F32)] if extra else []),
            pltpu.SemaphoreType.DMA((2 * count,)),
        ],
        14,
        4,
    )


def per_device(matrix, pattern_cols, pattern_counts):
    weights = jnp.array([1, 4, 16, 64], jnp.int32)
    code = jnp.sum(pattern_cols * weights, axis=2) + pattern_counts * 256
    core = lax.axis_index("col") % 2

    keep = lax.dynamic_slice_in_dim(matrix, HALF * core, HALF, 0)
    send = lax.dynamic_slice_in_dim(matrix, HALF * (1 - core), HALF, 0)
    halves = jnp.concatenate([keep, other_core(send)], axis=0)
    left_early, left_dense, left_late = gather(matrix, True, KINDS[0], lambda x: make_dense(code, True, x))
    right_early, right_dense, right_late = gather(halves, False, KINDS[1], lambda x: make_dense(code, False, x))
    left_last = make_dense(code, True, left_late)
    keep, send, *left = square(
        code, [left_early, left_late], [left_dense, left_last], right_early, right_dense, right_late
    )

    early, _, late = gather(keep + other_core(send), False, KINDS[2])
    part = times(code, left, early)[0]
    mine, other = times(code, left, late, part)
    return mine + other_core(other)


def solution(mesh):
    return jax.shard_map(
        per_device,
        mesh=mesh,
        in_specs=(P("row", None, "col"), P(), P()),
        out_specs=P("row", None, "col"),
        check_vma=False,
    )
```

```python
import jax
import jax.numpy as jnp
from jax import lax
from jax.experimental import pallas as pl
from jax.experimental.pallas import tpu as pltpu
from jax.sharding import PartitionSpec as P

ROWS = 8
HALF = ROWS // 2
BS = 64
RING = 4
KINDS = ("M", "M", "F")
SIDES = 8
VMEM = pl.BlockSpec(memory_space=pltpu.VMEM)
SMEM = pl.BlockSpec(memory_space=pltpu.SMEM)
BF16 = jnp.bfloat16
F32 = jnp.float32


def move(value, along_row, flip, shift):
    pairs = []
    for row in range(SIDES):
        for chip in range(SIDES):
            half, at = divmod(chip if along_row else row, RING)
            place = (half ^ flip) * RING + (at + shift) % RING
            target = (row, place) if along_row else (place, chip)
            for core in range(2):
                pairs.append(((row * SIDES + chip) * 2 + core, (target[0] * SIDES + target[1]) * 2 + core))
    return lax.ppermute(value, ("row", "col"), pairs)


def other_core(value):
    return lax.ppermute(value, "col", [(c, c ^ 1) for c in range(2 * SIDES)])


def whole(array, flip, shift):
    return [(array, 0, ROWS, 0)], flip, shift


def by_half(low, high, flip, first=(0, 0)):
    return [(low, first[0], HALF, 0), (high, first[1], HALF, HALF)], flip, 2


def gather(value, along_row, kind, use_early=None):
    step = lambda v, flip, shift: move(v, along_row, flip, shift)
    across, one, three = step(value, 1, 0), step(value, 0, 1), step(value, 0, 3)
    low = high = two = None
    if kind in ("P", "L7", "L8"):
        two = step(value, 0, 2)
        own_two = whole(two, 0, 2)
    elif kind == "W":
        two = step(one, 0, 1)
        own_two = whole(two, 0, 2)
    else:
        low, high = step(one[:HALF], 0, 1), step(three[HALF:], 0, 3)
        own_two = by_half(low, high, 0)
    early = [whole(value, 0, 0), whole(one, 0, 1), whole(three, 0, 3), own_two, whole(across, 1, 0)]
    used = None
    if use_early:
        used = list(use_early(early))
    g1, g3 = step(across, 0, 1), step(across, 0, 3)
    if kind in ("P", "W"):
        far_two = whole(step(two, 1, 0), 1, 2)
    elif kind == "F":
        far_two = by_half(step(low, 1, 0), step(high, 1, 0), 1)
    elif kind == "M":
        both = step(jnp.concatenate([low, high], axis=0), 1, 0)
        far_two = whole(both, 1, 2)
    elif kind == "L7":
        far_two = whole(step(g1, 0, 1), 1, 2)
    else:
        far_two = by_half(step(g1[:HALF], 0, 1), step(g3[HALF:], 0, 3), 1)
    late = [whole(g1, 1, 1), whole(g3, 1, 3), far_two]
    return early, used, late


def turned(half):
    return pltpu.roll(half, BS, 1)


VIEWS = ((0, 1), (1, 0), (2, 3), (3, 2))


def views_of(tile):
    first, second = tile[:, :128], tile[:, 128:]
    return first, turned(first), second, turned(second)


def slot_cols(code):
    return [jnp.where((code >> 8) > a, (code >> (2 * a)) & 3, 7) for a in range(4)]


def spread_masks(code):
    cols = slot_cols(code)
    low = lax.broadcasted_iota(jnp.int32, (16, 128), 1) < BS
    high = jnp.where(low, 0, 1)
    found = [jnp.where(low, cols[a], cols[b]) for a, b in VIEWS]
    return [[f == high + 2 * t for f in found] for t in range(2)]


def collect_masks(code):
    cols = slot_cols(code)
    low = lax.broadcasted_iota(jnp.int32, (16, 128), 1) < BS
    wanted = [jnp.where(low, cols[2 * u], cols[2 * u + 1]) for u in range(2)]
    return [[w == jnp.where(low, j, k) for j, k in VIEWS] for w in wanted]


def choose(masks, views):
    out = jnp.zeros((16, 128), F32)
    for mask, view in zip(masks, views):
        out = jnp.where(mask, view, out)
    return out


def position():
    panel = lax.axis_index("col")
    return lax.axis_index("row"), panel // 2, panel % 2


def put(tile, masks, hi_ref, lo_ref, at, first_row, first_col):
    for g in range(BS // 16):
        rows = slice(first_row + 16 * g, first_row + 16 * g + 16)
        views = views_of(tile[16 * g : 16 * g + 16, :])
        for t in range(2):
            cols = slice(first_col + 128 * t, first_col + 128 * t + 128)
            dense = choose(masks[t], views)
            hi = dense.astype(BF16)
            hi_ref[at, rows, cols] = hi
            lo_ref[at, rows, cols] = (dense - hi.astype(F32)).astype(BF16)


def source_of(place, flip, shift):
    half, spot = place // RING, place % RING
    return (half if flip == 0 else 1 - half) * RING + (spot - shift + RING) % RING


def unpack_left(shards, refs, code_ref, hi_ref, lo_ref, by_source):
    row, chip, core = position()
    for place, (pieces, flip, shift) in enumerate(shards):
        source = source_of(chip, flip, shift)
        for at, first, count, start in pieces:
            for n in range(count):
                i = start + n
                masks = spread_masks(code_ref[row * ROWS + i, 2 * source + core])
                put(refs[at][first + n], masks, hi_ref, lo_ref, source if by_source else place, BS * i, 0)


def unpack_right(shards, refs, code_ref, hi_ref, lo_ref, by_source):
    row, chip, core = position()
    for place, (pieces, flip, shift) in enumerate(shards):
        source = source_of(row, flip, shift)
        for at, first, count, start in pieces:
            for n in range(count):
                part, i = divmod(start + n, HALF)
                panel = 2 * chip + (core if part == 0 else 1 - core)
                masks = spread_masks(code_ref[source * ROWS + HALF * core + i, panel])
                at_place = source if by_source else place
                put(refs[at][first + n], masks, hi_ref, lo_ref, at_place, BS * i, 256 * part)


def multiply(left_hi, left_lo, right_hi, right_lo, count):
    lefts, rights = [], []
    for k in range(count):
        lefts += [left_hi[k], left_lo[k], left_hi[k]]
        rights += [right_hi[k], right_hi[k], right_lo[k]]
    return jnp.dot(jnp.concatenate(lefts, axis=1), jnp.concatenate(rights, axis=0), preferred_element_type=F32)


def collect(total, code_ref, part, i, finish, out_ref, at):
    row, chip, core = position()
    panel = 2 * chip + (core if part == 0 else 1 - core)
    masks = collect_masks(code_ref[row * ROWS + i, panel])
    for g in range(BS // 16):
        first = i * BS + 16 * g
        rows = pl.ds(first if isinstance(first, int) else pl.multiple_of(first, 16), 16)
        views = views_of(finish(total[rows, 256 * part : 256 * part + 256], row * ROWS * BS + first, panel * 256))
        for u in range(2):
            out_ref[at, 16 * g : 16 * g + 16, 128 * u : 128 * u + 128] = choose(masks[u], views)


def from_three(tile, first_row, first_col):
    at_row = first_row + lax.broadcasted_iota(jnp.int32, (16, 256), 0)
    at_col = first_col + lax.broadcasted_iota(jnp.int32, (16, 256), 1)
    return jnp.where(at_row == at_col, 3.0, 0.0) - tile


def flatten(shards):
    arrays, placed = [], []
    for pieces, flip, shift in shards:
        placed.append(([(len(arrays) + n, *piece[1:]) for n, piece in enumerate(pieces)], flip, shift))
        arrays += [piece[0] for piece in pieces]
    return arrays, placed


ANYWHERE = pl.BlockSpec(memory_space=pl.ANY)
SLOTS = jax.ShapeDtypeStruct((ROWS, BS, 256), F32)


def left_shape(count):
    return (count, ROWS * BS, 256)


def right_shape(count):
    return (count, HALF * BS, 512)


def call(kernel, inputs, in_specs, outs, out_specs, scratch, megabytes, microseconds):
    return pl.pallas_call(
        kernel,
        out_shape=outs,
        in_specs=in_specs,
        out_specs=out_specs,
        scratch_shapes=scratch,
        compiler_params=pltpu.CompilerParams(vmem_limit_bytes=megabytes * 2**20),
        cost_estimate=pl.CostEstimate(flops=0, bytes_accessed=microseconds * 3_000_000, transcendentals=0),
    )(*inputs)


def make_dense(code, along_row, shards):
    arrays, plan = flatten(shards)
    unpack, shape = (unpack_left, left_shape) if along_row else (unpack_right, right_shape)

    def kernel(code_ref, *refs):
        unpack(plan, refs, code_ref, refs[-2], refs[-1], False)

    outs = [jax.ShapeDtypeStruct(shape(len(shards)), BF16)] * 2
    return call(kernel, [code, *arrays], [SMEM] + [VMEM] * len(arrays), outs, [VMEM] * 2, [], 8, 2)


def finish_left(code, early, dense, shards):
    arrays, plan = flatten(shards)
    places = [(flip, shift) for _, flip, shift in early]

    def kernel(code_ref, *refs):
        outs = refs[-2:]
        _, chip, _ = position()
        unpack_left(plan, refs[2:-2], code_ref, *outs, True)
        for k, (flip, shift) in enumerate(places):
            source = source_of(chip, flip, shift)
            for here, out in zip(refs[:2], outs):
                out[source] = here[k]

    outs = [jax.ShapeDtypeStruct(left_shape(SIDES), BF16)] * 2
    specs = [SMEM] + [VMEM] * (2 + len(arrays))
    return call(kernel, [code, *dense, *arrays], specs, outs, [VMEM] * 2, [], 12, 3)


def square(code, left, right_lists, right_dense, last_shards):
    arrays, plan = flatten(last_shards)
    n_dense = 2 * len(right_dense)

    def kernel(code_ref, left_hi, left_lo, *refs):
        ready, refs = refs[:n_dense], refs[n_dense:]
        arrived, (keep_ref, send_ref, last_hi, last_lo, total) = refs[: len(arrays)], refs[len(arrays) :]
        row, _, core = position()
        unpack_right(plan, arrived, code_ref, last_hi, last_lo, False)
        ones, others = [], []
        sides = [(ready[2 * n], ready[2 * n + 1]) for n in range(len(right_lists))] + [(last_hi, last_lo)]
        for shards, (right_hi, right_lo) in zip([*right_lists, last_shards], sides):
            for k, (_, flip, shift) in enumerate(shards):
                source = source_of(row, flip, shift)
                ones += [left_hi[source], left_lo[source], left_hi[source]]
                others += [right_hi[k], right_hi[k], right_lo[k]]
        total[...] = jnp.dot(
            jnp.concatenate(ones, axis=1), jnp.concatenate(others, axis=0), preferred_element_type=F32
        )
        for part in range(2):
            for n in range(HALF):
                collect(total, code_ref, part, HALF * core + n, from_three, keep_ref, HALF * part + n)
                collect(
                    total, code_ref, part, HALF * (1 - core) + n, lambda t, *_: -t, send_ref, HALF * (1 - part) + n
                )

    return call(
        kernel,
        [code, *left, *[a for pair in right_dense for a in pair], *arrays],
        [SMEM] + [VMEM] * (2 + n_dense + len(arrays)),
        [SLOTS, SLOTS],
        [VMEM, VMEM],
        [
            *[pltpu.VMEM(right_shape(len(last_shards)), BF16)] * 2,
            pltpu.VMEM((ROWS * BS, 512), F32),
        ],
        20,
        8,
    )


def times(code, left, right_shards, before=None):
    arrays, plan = flatten(right_shards)
    n_in, count = len(arrays), len(right_shards)
    extra = [] if before is None else [before]

    def kernel(code_ref, far_hi, far_lo, *refs):
        arrived, refs = refs[:n_in], refs[n_in:]
        before_ref, refs = refs[: len(extra)], refs[len(extra) :]
        outs, refs = refs[: 1 + len(extra)], refs[1 + len(extra) :]
        *sides, sems = refs
        row, _, _ = position()
        loads = []
        for k, (_, flip, shift) in enumerate(plan):
            source = source_of(row, flip, shift)
            for n, far in enumerate((far_hi, far_lo)):
                loads.append(pltpu.make_async_copy(far.at[source], sides[n].at[k], sems.at[2 * k + n]))
        for m in loads:
            m.start()
        unpack_right(plan, arrived, code_ref, sides[2], sides[3], False)
        for m in loads:
            m.wait()
        if not extra:
            outs[0][...] = multiply(*sides[:4], count)
            return
        total = sides[4]
        total[...] = before_ref[0][...] + multiply(*sides[:4], count)
        for part in range(2):
            for i in range(ROWS):
                collect(total, code_ref, part, i, lambda t, *_: 0.5 * t, outs[part], i)

    dense = jax.ShapeDtypeStruct((ROWS * BS, 512), F32)
    return call(
        kernel,
        [code, *left, *arrays, *extra],
        [SMEM] + [ANYWHERE] * 2 + [VMEM] * (n_in + len(extra)),
        [SLOTS, SLOTS] if extra else [dense],
        [VMEM, VMEM] if extra else [VMEM],
        [
            *[pltpu.VMEM(left_shape(count), BF16)] * 2,
            *[pltpu.VMEM(right_shape(count), BF16)] * 2,
            *([pltpu.VMEM((ROWS * BS, 512), F32)] if extra else []),
            pltpu.SemaphoreType.DMA((2 * count,)),
        ],
        14,
        4,
    )


def per_device(matrix, pattern_cols, pattern_counts):
    weights = jnp.array([1, 4, 16, 64], jnp.int32)
    code = jnp.sum(pattern_cols * weights, axis=2) + pattern_counts * 256
    core = lax.axis_index("col") % 2

    keep = lax.dynamic_slice_in_dim(matrix, HALF * core, HALF, 0)
    send = lax.dynamic_slice_in_dim(matrix, HALF * (1 - core), HALF, 0)
    halves = jnp.concatenate([keep, other_core(send)], axis=0)
    left_early, left_dense, left_late = gather(matrix, True, KINDS[0], lambda x: make_dense(code, True, x))
    right_early, right_dense, right_late = gather(halves, False, KINDS[1], lambda x: make_dense(code, False, x))
    left = finish_left(code, left_early, left_dense, left_late)
    keep, send = square(code, left, [right_early], [right_dense], right_late)

    early, _, late = gather(keep + other_core(send), False, KINDS[2])
    part = times(code, left, early)[0]
    mine, other = times(code, left, late, part)
    return mine + other_core(other)


def solution(mesh):
    return jax.shard_map(
        per_device,
        mesh=mesh,
        in_specs=(P("row", None, "col"), P(), P()),
        out_specs=P("row", None, "col"),
        check_vma=False,
    )
```

```python
import jax
import jax.numpy as jnp
from jax import lax
from jax.experimental import pallas as pl
from jax.experimental.pallas import tpu as pltpu
from jax.sharding import PartitionSpec as P

ROWS = 8
HALF = ROWS // 2
BS = 64
RING = 4
KINDS = ("F3", "M", "F")
SIDES = 8
VMEM = pl.BlockSpec(memory_space=pltpu.VMEM)
SMEM = pl.BlockSpec(memory_space=pltpu.SMEM)
BF16 = jnp.bfloat16
F32 = jnp.float32


def move(value, along_row, flip, shift):
    pairs = []
    for row in range(SIDES):
        for chip in range(SIDES):
            half, at = divmod(chip if along_row else row, RING)
            place = (half ^ flip) * RING + (at + shift) % RING
            target = (row, place) if along_row else (place, chip)
            for core in range(2):
                pairs.append(((row * SIDES + chip) * 2 + core, (target[0] * SIDES + target[1]) * 2 + core))
    return lax.ppermute(value, ("row", "col"), pairs)


def other_core(value):
    return lax.ppermute(value, "col", [(c, c ^ 1) for c in range(2 * SIDES)])


def whole(array, flip, shift):
    return [(array, 0, ROWS, 0)], flip, shift


def by_half(low, high, flip, first=(0, 0)):
    return [(low, first[0], HALF, 0), (high, first[1], HALF, HALF)], flip, 2


def gather(value, along_row, kind, use_early=None):
    step = lambda v, flip, shift: move(v, along_row, flip, shift)
    across, one, three = step(value, 1, 0), step(value, 0, 1), step(value, 0, 3)
    low = high = two = None
    if kind in ("P", "L7", "L8"):
        two = step(value, 0, 2)
        own_two = whole(two, 0, 2)
    elif kind == "W":
        two = step(one, 0, 1)
        own_two = whole(two, 0, 2)
    else:
        low, high = step(one[:HALF], 0, 1), step(three[HALF:], 0, 3)
        own_two = by_half(low, high, 0)
    early = [whole(value, 0, 0), whole(one, 0, 1), whole(three, 0, 3), own_two, whole(across, 1, 0)]
    used = None
    if use_early:
        used = list(use_early(early))
    g1, g3 = step(across, 0, 1), step(across, 0, 3)
    if kind in ("P", "W"):
        far_two = whole(step(two, 1, 0), 1, 2)
    elif kind == "F":
        far_two = by_half(step(low, 1, 0), step(high, 1, 0), 1)
    elif kind == "M":
        both = step(jnp.concatenate([low, high], axis=0), 1, 0)
        far_two = whole(both, 1, 2)
    elif kind == "L7":
        far_two = whole(step(g1, 0, 1), 1, 2)
    else:
        far_two = by_half(step(g1[:HALF], 0, 1), step(g3[HALF:], 0, 3), 1)
    late = [whole(g1, 1, 1), whole(g3, 1, 3), far_two]
    return early, used, late


def turned(half):
    return pltpu.roll(half, BS, 1)


VIEWS = ((0, 1), (1, 0), (2, 3), (3, 2))


def views_of(tile):
    first, second = tile[:, :128], tile[:, 128:]
    return first, turned(first), second, turned(second)


def slot_cols(code):
    return [jnp.where((code >> 8) > a, (code >> (2 * a)) & 3, 7) for a in range(4)]


def spread_masks(code):
    cols = slot_cols(code)
    low = lax.broadcasted_iota(jnp.int32, (16, 128), 1) < BS
    high = jnp.where(low, 0, 1)
    found = [jnp.where(low, cols[a], cols[b]) for a, b in VIEWS]
    return [[f == high + 2 * t for f in found] for t in range(2)]


def collect_masks(code):
    cols = slot_cols(code)
    low = lax.broadcasted_iota(jnp.int32, (16, 128), 1) < BS
    wanted = [jnp.where(low, cols[2 * u], cols[2 * u + 1]) for u in range(2)]
    return [[w == jnp.where(low, j, k) for j, k in VIEWS] for w in wanted]


def choose(masks, views):
    out = jnp.zeros((16, 128), F32)
    for mask, view in zip(masks, views):
        out = jnp.where(mask, view, out)
    return out


def position():
    panel = lax.axis_index("col")
    return lax.axis_index("row"), panel // 2, panel % 2


def put(tile, masks, hi_ref, lo_ref, at, first_row, first_col):
    for g in range(BS // 16):
        rows = slice(first_row + 16 * g, first_row + 16 * g + 16)
        views = views_of(tile[16 * g : 16 * g + 16, :])
        for t in range(2):
            cols = slice(first_col + 128 * t, first_col + 128 * t + 128)
            dense = choose(masks[t], views)
            hi = dense.astype(BF16)
            hi_ref[at, rows, cols] = hi
            lo_ref[at, rows, cols] = (dense - hi.astype(F32)).astype(BF16)


def source_of(place, flip, shift):
    half, spot = place // RING, place % RING
    return (half if flip == 0 else 1 - half) * RING + (spot - shift + RING) % RING


def unpack_left(shards, refs, code_ref, hi_ref, lo_ref, by_source):
    row, chip, core = position()
    for place, (pieces, flip, shift) in enumerate(shards):
        source = source_of(chip, flip, shift)
        for at, first, count, start in pieces:
            for n in range(count):
                i = start + n
                masks = spread_masks(code_ref[row * ROWS + i, 2 * source + core])
                put(refs[at][first + n], masks, hi_ref, lo_ref, source if by_source else place, BS * i, 0)


def unpack_right(shards, refs, code_ref, hi_ref, lo_ref, by_source):
    row, chip, core = position()
    for place, (pieces, flip, shift) in enumerate(shards):
        source = source_of(row, flip, shift)
        for at, first, count, start in pieces:
            for n in range(count):
                part, i = divmod(start + n, HALF)
                panel = 2 * chip + (core if part == 0 else 1 - core)
                masks = spread_masks(code_ref[source * ROWS + HALF * core + i, panel])
                at_place = source if by_source else place
                put(refs[at][first + n], masks, hi_ref, lo_ref, at_place, BS * i, 256 * part)


def multiply(left_hi, left_lo, right_hi, right_lo, count):
    lefts, rights = [], []
    for k in range(count):
        lefts += [left_hi[k], left_lo[k], left_hi[k]]
        rights += [right_hi[k], right_hi[k], right_lo[k]]
    return jnp.dot(jnp.concatenate(lefts, axis=1), jnp.concatenate(rights, axis=0), preferred_element_type=F32)


def collect(total, code_ref, part, i, finish, out_ref, at):
    row, chip, core = position()
    panel = 2 * chip + (core if part == 0 else 1 - core)
    masks = collect_masks(code_ref[row * ROWS + i, panel])
    for g in range(BS // 16):
        first = i * BS + 16 * g
        rows = pl.ds(first if isinstance(first, int) else pl.multiple_of(first, 16), 16)
        views = views_of(finish(total[rows, 256 * part : 256 * part + 256], row * ROWS * BS + first, panel * 256))
        for u in range(2):
            out_ref[at, 16 * g : 16 * g + 16, 128 * u : 128 * u + 128] = choose(masks[u], views)


def from_three(tile, first_row, first_col):
    at_row = first_row + lax.broadcasted_iota(jnp.int32, (16, 256), 0)
    at_col = first_col + lax.broadcasted_iota(jnp.int32, (16, 256), 1)
    return jnp.where(at_row == at_col, 3.0, 0.0) - tile


def flatten(shards):
    arrays, placed = [], []
    for pieces, flip, shift in shards:
        placed.append(([(len(arrays) + n, *piece[1:]) for n, piece in enumerate(pieces)], flip, shift))
        arrays += [piece[0] for piece in pieces]
    return arrays, placed


ANYWHERE = pl.BlockSpec(memory_space=pl.ANY)
SLOTS = jax.ShapeDtypeStruct((ROWS, BS, 256), F32)


def left_shape(count):
    return (count, ROWS * BS, 256)


def right_shape(count):
    return (count, HALF * BS, 512)


def call(kernel, inputs, in_specs, outs, out_specs, scratch, megabytes, microseconds):
    return pl.pallas_call(
        kernel,
        out_shape=outs,
        in_specs=in_specs,
        out_specs=out_specs,
        scratch_shapes=scratch,
        compiler_params=pltpu.CompilerParams(vmem_limit_bytes=megabytes * 2**20),
        cost_estimate=pl.CostEstimate(flops=0, bytes_accessed=microseconds * 3_000_000, transcendentals=0),
    )(*inputs)


def make_dense(code, along_row, shards):
    arrays, plan = flatten(shards)
    unpack, shape = (unpack_left, left_shape) if along_row else (unpack_right, right_shape)

    def kernel(code_ref, *refs):
        unpack(plan, refs, code_ref, refs[-2], refs[-1], False)

    outs = [jax.ShapeDtypeStruct(shape(len(shards)), BF16)] * 2
    return call(kernel, [code, *arrays], [SMEM] + [VMEM] * len(arrays), outs, [VMEM] * 2, [], 8, 2)


def finish_left(code, early, dense, shards):
    arrays, plan = flatten(shards)
    places = [(flip, shift) for _, flip, shift in early]

    def kernel(code_ref, *refs):
        outs = refs[-2:]
        _, chip, _ = position()
        unpack_left(plan, refs[2:-2], code_ref, *outs, True)
        for k, (flip, shift) in enumerate(places):
            source = source_of(chip, flip, shift)
            for here, out in zip(refs[:2], outs):
                out[source] = here[k]

    outs = [jax.ShapeDtypeStruct(left_shape(SIDES), BF16)] * 2
    specs = [SMEM] + [VMEM] * (2 + len(arrays))
    return call(kernel, [code, *dense, *arrays], specs, outs, [VMEM] * 2, [], 12, 3)


def square(code, left, right_lists, right_dense, last_shards):
    arrays, plan = flatten(last_shards)
    n_dense = 2 * len(right_dense)

    def kernel(code_ref, left_hi, left_lo, *refs):
        ready, refs = refs[:n_dense], refs[n_dense:]
        arrived, (keep_ref, send_ref, last_hi, last_lo, total) = refs[: len(arrays)], refs[len(arrays) :]
        row, _, core = position()
        unpack_right(plan, arrived, code_ref, last_hi, last_lo, False)
        ones, others = [], []
        sides = [(ready[2 * n], ready[2 * n + 1]) for n in range(len(right_lists))] + [(last_hi, last_lo)]
        for shards, (right_hi, right_lo) in zip([*right_lists, last_shards], sides):
            for k, (_, flip, shift) in enumerate(shards):
                source = source_of(row, flip, shift)
                ones += [left_hi[source], left_lo[source], left_hi[source]]
                others += [right_hi[k], right_hi[k], right_lo[k]]
        total[...] = jnp.dot(
            jnp.concatenate(ones, axis=1), jnp.concatenate(others, axis=0), preferred_element_type=F32
        )
        for part in range(2):
            for n in range(HALF):
                collect(total, code_ref, part, HALF * core + n, from_three, keep_ref, HALF * part + n)
                collect(
                    total, code_ref, part, HALF * (1 - core) + n, lambda t, *_: -t, send_ref, HALF * (1 - part) + n
                )

    return call(
        kernel,
        [code, *left, *[a for pair in right_dense for a in pair], *arrays],
        [SMEM] + [VMEM] * (2 + n_dense + len(arrays)),
        [SLOTS, SLOTS],
        [VMEM, VMEM],
        [
            *[pltpu.VMEM(right_shape(len(last_shards)), BF16)] * 2,
            pltpu.VMEM((ROWS * BS, 512), F32),
        ],
        20,
        8,
    )


def times(code, left, right_shards, before=None):
    arrays, plan = flatten(right_shards)
    n_in, count = len(arrays), len(right_shards)
    extra = [] if before is None else [before]

    def kernel(code_ref, far_hi, far_lo, *refs):
        arrived, refs = refs[:n_in], refs[n_in:]
        before_ref, refs = refs[: len(extra)], refs[len(extra) :]
        outs, refs = refs[: 1 + len(extra)], refs[1 + len(extra) :]
        *sides, sems = refs
        row, _, _ = position()
        loads = []
        for k, (_, flip, shift) in enumerate(plan):
            source = source_of(row, flip, shift)
            for n, far in enumerate((far_hi, far_lo)):
                loads.append(pltpu.make_async_copy(far.at[source], sides[n].at[k], sems.at[2 * k + n]))
        for m in loads:
            m.start()
        unpack_right(plan, arrived, code_ref, sides[2], sides[3], False)
        for m in loads:
            m.wait()
        if not extra:
            outs[0][...] = multiply(*sides[:4], count)
            return
        total = sides[4]
        total[...] = before_ref[0][...] + multiply(*sides[:4], count)
        for part in range(2):
            for i in range(ROWS):
                collect(total, code_ref, part, i, lambda t, *_: 0.5 * t, outs[part], i)

    dense = jax.ShapeDtypeStruct((ROWS * BS, 512), F32)
    return call(
        kernel,
        [code, *left, *arrays, *extra],
        [SMEM] + [ANYWHERE] * 2 + [VMEM] * (n_in + len(extra)),
        [SLOTS, SLOTS] if extra else [dense],
        [VMEM, VMEM] if extra else [VMEM],
        [
            *[pltpu.VMEM(left_shape(count), BF16)] * 2,
            *[pltpu.VMEM(right_shape(count), BF16)] * 2,
            *([pltpu.VMEM((ROWS * BS, 512), F32)] if extra else []),
            pltpu.SemaphoreType.DMA((2 * count,)),
        ],
        14,
        4,
    )


def per_device(matrix, pattern_cols, pattern_counts):
    weights = jnp.array([1, 4, 16, 64], jnp.int32)
    code = jnp.sum(pattern_cols * weights, axis=2) + pattern_counts * 256
    core = lax.axis_index("col") % 2

    keep = lax.dynamic_slice_in_dim(matrix, HALF * core, HALF, 0)
    send = lax.dynamic_slice_in_dim(matrix, HALF * (1 - core), HALF, 0)
    halves = jnp.concatenate([keep, other_core(send)], axis=0)
    left_early, left_dense, left_late = gather(matrix, True, KINDS[0], lambda x: make_dense(code, True, x))
    right_early, right_dense, right_late = gather(halves, False, KINDS[1], lambda x: make_dense(code, False, x))
    left = finish_left(code, left_early, left_dense, left_late)
    keep, send = square(code, left, [right_early], [right_dense], right_late)

    early, _, late = gather(keep + other_core(send), False, KINDS[2])
    part = times(code, left, early)[0]
    mine, other = times(code, left, late, part)
    return mine + other_core(other)


def solution(mesh):
    return jax.shard_map(
        per_device,
        mesh=mesh,
        in_specs=(P("row", None, "col"), P(), P()),
        out_specs=P("row", None, "col"),
        check_vma=False,
    )
```
